256 devices in a mesh: store: 64 (over z, y, core), tp: 4 (over x).
Axes of the slice: x: 4, y: 4, z: 8, core: 2. Of those that a mesh axis runs over, the one named last changes fastest.
Arguments:
- query_embeds: bfloat16 [128, 16, 4096], P('store', None, 'tp'), may hold values from -6 to 6
- passage_embeds: bfloat16 [128, 32, 4096], P('store', None, 'tp'), may hold values from -6 to 6
- passage_lengths: int32 [128], P('store'), may hold values from 1 to 32, as said below
- cand_passage: int32 [1536], P('store'), may hold values from 0 to 127, as said below
- norm_gain: bfloat16 [4096], replicated, may hold values from 0.099609375 to 1.8984375
- w_qkv: bfloat16 [4096, 16, 384], P(None, 'tp'), may hold values from -1 to 1
Outputs:
- query_attn: bfloat16 [128, 16, 2048], P('store', None, 'tp')
- passage_attn: bfloat16 [1536, 32, 2048], P('store', None, 'tp')
The draws below stay inside these ranges and needn't reach their ends.
Inputs may be any that keep to these rules, and one draw needn't show every extreme that they name: `cand_passage`: passage id p is held by store index p // 2 at position p % 2. Among the 24 pairs of one store index, the passages come from as many different store indices as possible, and no store index holds the passages of more than 1 of them. `passage_lengths`: some passage has 32 tokens.
All inputs are finite; a program needn't handle non-finite values.
Results may differ from the reference program's by a relative error of at most 0.023.
The reference program's roundings to bfloat16 on the way count: a program that leaves them out, or rounds other values in their place, can miss the bound.
Values may be sent and summed in bfloat16 or wider, within the bound.
A program may use at most 128 MiB of HBM per device.

```python
import math
import jax
import jax.numpy as jnp
from jax import lax

D = 4096
HEADS = 16
HD = 128
QLEN = 16
PLEN = 32
CANDS = 12
PASS_DEV = 2
QUERIES = 128
PAIRS_DEV = 24
PAIRS = 1536
PASSAGES = 128


def draw_passage_lengths(key, part):
    first_key, second_key = jax.random.split(jax.random.fold_in(key, 11))
    lengths = jax.random.randint(first_key, (PASSAGES,), 1, PLEN + 1)
    marked = jax.random.randint(second_key, (), 0, PASSAGES)
    return jnp.where(jnp.arange(PASSAGES) == marked, PLEN, lengths).astype(jnp.int32)


def draw_cand_passage(key, part):
    first_key, second_key = jax.random.split(jax.random.fold_in(key, 23))
    groups = PAIRS // PAIRS_DEV
    shards = PASSAGES // PASS_DEV
    group_keys = jax.random.split(first_key, groups)
    orders = jax.vmap(lambda one_key: jax.random.permutation(one_key, shards))(group_keys)
    holders = orders[:, jnp.arange(PAIRS_DEV) % shards]
    positions = jax.random.randint(second_key, (groups, PAIRS_DEV), 0, PASS_DEV)
    return (holders * PASS_DEV + positions).reshape(PAIRS).astype(jnp.int32)


def draw_w_qkv(key, part):
    base = jax.random.normal(jax.random.fold_in(key, 37), (D, HEADS, 3 * HD), jnp.float32)
    base = jnp.clip(base, -6.0, 6.0) * D ** (-0.5)
    return jnp.clip(base, -1.0, 1.0).astype(jnp.bfloat16)


def shard_levels(stream_key, dims, cuts, smallest, top_value):
    gain = 1.0
    for axis_at, shards_of in cuts:
        heights = jax.random.uniform(jax.random.fold_in(jax.random.fold_in(stream_key, 6), axis_at), (shards_of,), jnp.float32, smallest / len(cuts), top_value / len(cuts))
        gain = gain * jnp.repeat(jnp.exp(heights), dims[axis_at] // shards_of).reshape((-1,) + (1,) * (len(dims) - 1 - axis_at))
    return gain


def noise(key, dims, scale, most, pieces=(), held_as=jnp.bfloat16):
    result = scale * jax.random.normal(key, dims, jnp.float32)
    if pieces:
        result = result * shard_levels(key, dims, pieces, -0.22, 0.18)
    return jnp.clip(result, -most, most).astype(held_as)


def setup_inputs(seed: int = 0) -> dict:
    keys = jax.random.split(jax.random.key(seed), 7)
    return {
        "query_embeds": noise(keys[0], (QUERIES, QLEN, D), 1.0, 6.0, ((0, 64), (2, 4))),
        "passage_embeds": noise(keys[1], (PASSAGES, PLEN, D), 1.0, 6.0, ((0, 64), (2, 4))),
        "passage_lengths": draw_passage_lengths(jax.random.fold_in(keys[6], 71), 0),
        "cand_passage": draw_cand_passage(jax.random.fold_in(keys[6], 71), 0),
        "norm_gain": jnp.clip(1.0 + 0.18 * jax.random.normal(keys[4], (D,), jnp.float32), 0.099609375, 1.8984375).astype(jnp.bfloat16),
        "w_qkv": draw_w_qkv(jax.random.fold_in(keys[6], 71), 0),
    }


def rms_rows(rows, norm_gain):
    values = rows.astype(jnp.float32)
    meansq = lax.optimization_barrier(jnp.mean(values * values, axis=-1, keepdims=True))
    scaled = values * lax.rsqrt(meansq + 1e-05) * norm_gain.astype(jnp.float32)
    return scaled.astype(jnp.bfloat16)

def rotate_parts(raw, positions, head_dim):
    half_dim = head_dim // 2
    inverse = jnp.exp(jnp.arange(half_dim, dtype=jnp.float32) * (-2.0 * math.log(10000.0) / head_dim))
    angles = positions[:, None] * inverse[None, :]
    cosine = jnp.cos(angles)[:, None, :]
    sine_part = jnp.sin(angles)[:, None, :]

    def turned(block):
        first = block[..., :half_dim]
        second = block[..., half_dim:]
        return jnp.concatenate([first * cosine - second * sine_part, second * cosine + first * sine_part], axis=-1)
    queries = turned(raw[..., :head_dim])
    keyset = turned(raw[..., head_dim:2 * head_dim])
    values = raw[..., 2 * head_dim:]
    return jnp.concatenate([queries, keyset, values], axis=-1).astype(jnp.bfloat16)

def project(rows, positions, norm_gain, weights_flat, heads, head_dim):
    normed = rms_rows(rows, norm_gain)
    raw = jnp.dot(normed, weights_flat, preferred_element_type=jnp.float32)
    raw = raw.reshape(rows.shape[0], heads, 3 * head_dim)
    return rotate_parts(raw, positions, head_dim)

def softmax_rounded(scores, allowed):
    masked = jnp.where(allowed, scores, jnp.float32(-1e+30))
    peak = lax.optimization_barrier(jnp.max(masked, axis=-1, keepdims=True))
    expon = jnp.where(allowed, jnp.exp(masked - peak), jnp.float32(0.0))
    return (expon / lax.optimization_barrier(jnp.sum(expon, axis=-1, keepdims=True))).astype(jnp.bfloat16)

def attend_queries(query_qkv, head_dim):
    count, query_len, heads = (query_qkv.shape[0], query_qkv.shape[1], query_qkv.shape[2])
    scale = head_dim ** (-0.5)
    qparts = query_qkv[..., :head_dim].astype(jnp.float32)
    kparts = query_qkv[..., head_dim:2 * head_dim].astype(jnp.float32)
    vparts = query_qkv[..., 2 * head_dim:].astype(jnp.float32)
    scores = jnp.einsum('bqhd,bkhd->bhqk', qparts, kparts) * scale
    steps_row = jnp.arange(query_len, dtype=jnp.int32)
    allowed = steps_row[:, None] >= steps_row[None, :]
    weights = softmax_rounded(scores, allowed[None, None])
    output = jnp.einsum('bhqk,bkhd->bqhd', weights.astype(jnp.float32), vparts)
    return output.reshape(count, query_len, heads * head_dim).astype(jnp.bfloat16)

def attend_pairs(query_qkv, pair_qkv, pair_lengths, head_dim, cands):
    query_len = query_qkv.shape[1]
    pairs, passage_len, heads = (pair_qkv.shape[0], pair_qkv.shape[1], pair_qkv.shape[2])
    scale = head_dim ** (-0.5)
    repeated = jnp.repeat(query_qkv, cands, axis=0)
    keyset = jnp.concatenate([repeated[..., head_dim:2 * head_dim], pair_qkv[..., head_dim:2 * head_dim]], axis=1)
    values = jnp.concatenate([repeated[..., 2 * head_dim:], pair_qkv[..., 2 * head_dim:]], axis=1)
    scores = jnp.einsum('bihd,bthd->bhit', pair_qkv[..., :head_dim].astype(jnp.float32), keyset.astype(jnp.float32)) * scale
    column = jnp.arange(query_len + passage_len, dtype=jnp.int32) - query_len
    row_index = jnp.arange(passage_len, dtype=jnp.int32)
    allowed = (column[None, None, :] < 0) | (column[None, None, :] <= row_index[None, :, None]) & (column[None, None, :] < pair_lengths[:, None, None])
    weights = softmax_rounded(scores, allowed[:, None])
    output = jnp.einsum('bhit,bthd->bihd', weights.astype(jnp.float32), values.astype(jnp.float32))
    live = row_index[None, :] < pair_lengths[:, None]
    output = jnp.where(live[:, :, None, None], output, jnp.float32(0.0))
    return output.reshape(pairs, passage_len, heads * head_dim).astype(jnp.bfloat16)

def reference(query_embeds, passage_embeds, passage_lengths, cand_passage, norm_gain, w_qkv):
    weights_flat = w_qkv.reshape(D, HEADS * 3 * HD)
    query_rows = query_embeds.reshape(QUERIES * QLEN, D)
    query_pos = jnp.tile(jnp.arange(QLEN, dtype=jnp.float32), QUERIES)
    query_qkv = project(query_rows, query_pos, norm_gain, weights_flat, HEADS, HD).reshape(QUERIES, QLEN, HEADS, 3 * HD)
    passage_rows = passage_embeds.reshape(PASSAGES * PLEN, D)
    passage_pos = QLEN + jnp.tile(jnp.arange(PLEN, dtype=jnp.float32), PASSAGES)
    passage_qkv = project(passage_rows, passage_pos, norm_gain, weights_flat, HEADS, HD).reshape(PASSAGES, PLEN, HEADS, 3 * HD)
    query_attn = attend_queries(query_qkv, HD)

    def one_query(inputs):
        own_qkv, chosen = inputs
        return attend_pairs(own_qkv[None], passage_qkv[chosen], passage_lengths[chosen], HD, CANDS)
    per_query = lax.map(one_query, (query_qkv, cand_passage.reshape(QUERIES, CANDS)))
    passage_attn = per_query.reshape(PAIRS, PLEN, HEADS * HD)
    return (query_attn, passage_attn)
```

```python
import functools
import math

import jax
import jax.numpy as jnp
import numpy as np
from jax import lax
from jax.experimental import pallas as pl
from jax.experimental.pallas import tpu as pltpu
from jax.sharding import PartitionSpec as P

MESH = pl.DeviceIdType.MESH
NZ, NY = 8, 4
D, DPART, HEADS, HD = 4096, 1024, 4, 128
QLEN, PLEN, CANDS, PAIRS = 16, 32, 12, 24
PROWS, QROWS = 2 * PLEN, 2 * QLEN
A_TILES = 5 * 4 + 1
B_TILES = 3 * 4 + 1
A_AT = {"q0": 0, "o0": 1, "q1": 2, "o1": 3, "q2": 4}
B_AT = {"o2": 0, "q3": 1, "o3": 2}
DEAD = 1e30
W_CUTS = 8
Z_GROUPS = ((0, 1), (1, 2), (3, 2), (5, 2), (7, 1))
Y_GROUPS = ((0, 1), (1, 2), (3, 1))
N_SEMS = 160


def tables():
    inverse = np.exp(np.arange(64, dtype=np.float32) * np.float32(-2.0 * math.log(10000.0) / HD))
    where = np.concatenate([np.tile(QLEN + np.arange(PLEN), 2), np.tile(np.arange(QLEN), 2)])
    angles = (where.astype(np.float32)[:, None] * inverse[None, :].astype(np.float32)).astype(np.float64)
    cosine, sine = np.cos(angles), np.sin(angles)
    return np.stack(
        [np.concatenate([cosine, cosine], 1), np.concatenate([-sine, sine], 1)]
    ).astype(np.float32)


def dot_nt(a, b):
    return lax.dot_general(a, b, (((1,), (1,)), ((), ())), preferred_element_type=jnp.float32)


def dot_tn(a, b):
    return lax.dot_general(a, b, (((0,), (0,)), ((), ())), preferred_element_type=jnp.float32)


def kernel(
    len_ref, cand_ref, q_ref, p_ref, gain_ref, table_ref, w_ref, qo_ref, po_ref,
    px, qx, wv, wr, acc, gain_wide, ga, gb, got_q, got_o, stats, qk, qv, w_sem, send, recv,
):
    store, me_x = lax.axis_index("store"), lax.axis_index("tp")
    z, y, core = lax.div(store, 8), lax.rem(lax.div(store, 2), 4), lax.rem(store, 2)
    scale = HD ** (-0.5)

    def at(zz, yy, cc, xx):
        return {"store": (lax.rem(zz, NZ) * NY + lax.rem(yy, NY)) * 2 + cc, "tp": lax.rem(xx, 4)}

    z_up, z_down = at(z + 1, y, core, me_x), at(z + NZ - 1, y, core, me_x)
    y_up, y_down = at(z, y + 1, core, me_x), at(z, y + NY - 1, core, me_x)
    x_up, x_down = at(z, y, core, me_x + 1), at(z, y, core, me_x + 3)
    sibling = at(z, y, 1 - core, me_x)
    even = core == 0
    z_last = at(jnp.where(even, z + 1, z + NZ - 1), y, core, me_x)
    y_last = at(z, jnp.where(even, y + 1, y + NY - 1), core, me_x)

    made = []

    def copy(src, dst, device):
        k = len(made)
        c = pltpu.make_async_remote_copy(
            src, dst, send.at[k], recv.at[k], device_id=device, device_id_type=MESH
        )
        made.append(c)
        c.start()
        return c

    cut = D // W_CUTS
    w_copies = [
        pltpu.make_async_copy(w_ref.at[pl.ds(i * cut, cut)], wv.at[pl.ds(i * cut, cut)], w_sem.at[i])
        for i in range(W_CUTS)
    ]
    for c in w_copies:
        c.start()

    barrier = pltpu.get_barrier_semaphore()
    near = (z_up, z_down, y_up, y_down, x_up, x_down, sibling)
    for device in near:
        pl.semaphore_signal(barrier, inc=1, device_id=device, device_id_type=MESH)
    pl.semaphore_wait(barrier, len(near))

    left, right = lax.rem(me_x + 3, 4), lax.rem(me_x + 1, 4)
    p_hop = [copy(p_ref, px.at[me_x], x_up), copy(p_ref, px.at[me_x], x_down)]
    q_hop = [copy(q_ref, qx.at[me_x], x_up), copy(q_ref, qx.at[me_x], x_down)]
    for c in range(4):
        gain_wide[c] = gain_ref[pl.ds(c * DPART, DPART)].astype(jnp.float32).reshape(1, DPART)
    px[me_x] = p_ref[...]
    qx[me_x] = q_ref[...]

    for i, c in enumerate(w_copies):
        c.wait()

        @pl.loop(0, cut // 64)
        def _(j):
            row = pl.multiple_of(i * cut + j * 64, 64)
            for h in range(HEADS):
                wr[pl.ds(row, 64), h * 384 : (h + 1) * 384] = wv[pl.ds(row, 64), h, :]

    for c in p_hop:
        c.wait_recv()
    low, high = pl.ds(0, PLEN), pl.ds(PLEN, PLEN)
    p_far = [
        copy(px.at[left, low], px.at[left, low], x_up),
        copy(px.at[right, high], px.at[right, high], x_down),
    ]
    for c in q_hop:
        c.wait_recv()
    low, high = pl.ds(0, QLEN), pl.ds(QLEN, QLEN)
    q_far = [
        copy(qx.at[left, low], qx.at[left, low], x_up),
        copy(qx.at[right, high], qx.at[right, high], x_down),
    ]

    def project(rows_ref, rows):
        total = jnp.zeros((rows, 1), jnp.float32)
        for c in range(4):
            values = rows_ref[c].astype(jnp.float32)
            total = total + jnp.sum(values * values, axis=-1, keepdims=True)
        inverse = lax.rsqrt(total * (1.0 / D) + 1e-05)
        acc[pl.ds(0, rows), :] = jnp.zeros((rows, HEADS * 384), jnp.float32)

        @pl.loop(0, 4)
        def _(c):
            values = rows_ref[c].astype(jnp.float32)
            gain = gain_wide[c]
            normed = (values * inverse * gain).astype(jnp.bfloat16)
            depth = pl.ds(pl.multiple_of(c * DPART, DPART), DPART)
            acc[pl.ds(0, rows), :] += jnp.dot(
                normed, wr[depth, :], preferred_element_type=jnp.float32
            )

    def turned(part, rows, row0):
        cosine, sine = table_ref[0, pl.ds(row0, rows), :], table_ref[1, pl.ds(row0, rows), :]
        return (part * cosine + pltpu.roll(part, 64, 1) * sine).astype(jnp.bfloat16)

    for c in p_far:
        c.wait_recv()
    project(px, PROWS)

    row = lax.broadcasted_iota(jnp.int32, (PROWS, PROWS), 0)
    col = lax.broadcasted_iota(jnp.int32, (PROWS, PROWS), 1)
    seen = (col <= row) & (lax.div(row, PLEN) == lax.div(col, PLEN))
    out_row = lax.broadcasted_iota(jnp.int32, (PROWS, HD), 0)
    len0, len1 = len_ref[0], len_ref[1]
    live = lax.rem(out_row, PLEN) < jnp.where(out_row < PLEN, len0, len1)
    key_row = lax.broadcasted_iota(jnp.int32, (PLEN, 128), 0)
    token = lax.rem(lax.broadcasted_iota(jnp.int32, (PLEN, 128), 1), PLEN)
    seen_t = key_row <= token
    token_row = lax.rem(lax.broadcasted_iota(jnp.int32, (1, 128), 1), PLEN)
    stat_row = lax.broadcasted_iota(jnp.int32, (16, 128), 0)
    stat = [jnp.zeros((16, 128), jnp.float32), jnp.zeros((16, 128), jnp.float32)]

    def put(name, value):
        where, slots = (ga, A_AT) if name in A_AT else (gb, B_AT)
        where[0, pl.ds(slots[name] * 4, 4)] = value.reshape(4, 16, HD)

    for h in range(HEADS):
        queries = turned(acc[pl.ds(0, PROWS), h * 384 : h * 384 + 128], PROWS, 0)
        keys = turned(acc[pl.ds(0, PROWS), h * 384 + 128 : h * 384 + 256], PROWS, 0)
        values = acc[pl.ds(0, PROWS), h * 384 + 256 : h * 384 + 384].astype(jnp.bfloat16)
        scores = jnp.where(seen, dot_nt(queries, keys) * scale, -1e30)
        peak = jnp.max(scores, axis=-1, keepdims=True)
        expon = jnp.where(seen, jnp.exp(scores - peak), 0.0)
        weights = (expon / jnp.sum(expon, axis=-1, keepdims=True)).astype(jnp.bfloat16)
        own = jnp.dot(weights, values, preferred_element_type=jnp.float32)
        put(f"q{h}", queries)
        put(f"o{h}", jnp.where(live, own, 0.0).astype(jnp.bfloat16))
        for j in range(2):
            some = queries[j * PLEN : (j + 1) * PLEN]
            turned_scores = dot_nt(
                keys[j * PLEN : (j + 1) * PLEN], jnp.concatenate([some] * 4, axis=0)
            )
            turned_scores = jnp.where(seen_t, turned_scores * scale, -1e30)
            top = jnp.max(turned_scores, axis=0, keepdims=True)
            mass = jnp.sum(jnp.where(seen_t, jnp.exp(turned_scores - top), 0.0), axis=0, keepdims=True)
            level = jnp.where(token_row < (len0, len1)[j], top + jnp.log(mass), DEAD)
            coarse = level.astype(jnp.bfloat16).astype(jnp.float32)
            at_row = j * 8 + 2 * (h % 2)
            block = stat[h // 2]
            block = jnp.where(stat_row == at_row, coarse, block)
            stat[h // 2] = jnp.where(stat_row == at_row + 1, level - coarse, block)
    ga[0, A_TILES - 1] = stat[0].astype(jnp.bfloat16)
    gb[0, B_TILES - 1] = stat[1].astype(jnp.bfloat16)

    def a_slots(half, ys, zs, n):
        return ga.at[pl.ds(half * 32 + ys * 8 + zs, n)]

    def b_slots(half, zs, ys, n):
        return gb.at[pl.ds(half * 32 + zs * 4 + ys, n)]

    def a_z(step):
        if step == 3:
            return [copy(a_slots(0, 0, jnp.where(even, 6, 5), 1), a_slots(0, 0, 7, 1), z_last)]
        up, down = (0, 2, 4)[step], (0, 1, 3)[step]
        return [
            copy(a_slots(0, 0, up, 1), a_slots(0, 0, 2 * step + 2, 1), z_up),
            copy(a_slots(0, 0, down, 1), a_slots(0, 0, 2 * step + 1, 1), z_down),
        ]

    def a_y(g):
        zs, n = Z_GROUPS[g]
        return [
            copy(a_slots(0, 0, zs, n), a_slots(0, 2, zs, n), y_up),
            copy(a_slots(0, 0, zs, n), a_slots(0, 1, zs, n), y_down),
        ]

    def a_y_last(g):
        zs, n = Z_GROUPS[g]
        return [copy(a_slots(0, jnp.where(even, 2, 1), zs, n), a_slots(0, 3, zs, n), y_last)]

    def a_sib(ys, g):
        zs, n = Z_GROUPS[g]
        return copy(a_slots(0, ys, zs, n), a_slots(1, ys, zs, n), sibling)

    def b_y():
        return [
            copy(b_slots(0, 0, 0, 1), b_slots(0, 0, 2, 1), y_up),
            copy(b_slots(0, 0, 0, 1), b_slots(0, 0, 1, 1), y_down),
        ]

    def b_y_last():
        return [copy(b_slots(0, 0, jnp.where(even, 2, 1), 1), b_slots(0, 0, 3, 1), y_last)]

    def b_z(e, step):
        ys, n = Y_GROUPS[e]
        if step == 3:
            return [copy(b_slots(0, jnp.where(even, 6, 5), ys, n), b_slots(0, 7, ys, n), z_last)]
        up, down = (0, 2, 4)[step], (0, 1, 3)[step]
        return [
            copy(b_slots(0, up, ys, n), b_slots(0, 2 * step + 2, ys, n), z_up),
            copy(b_slots(0, down, ys, n), b_slots(0, 2 * step + 1, ys, n), z_down),
        ]

    def b_sib(g):
        zs, n = Z_GROUPS[g]
        return copy(b_slots(0, zs, 0, 4 * n), b_slots(1, zs, 0, 4 * n), sibling)

    def arrived(copies):
        for c in copies:
            c.wait_recv()

    a_sibs, b_sibs = [], []
    az = {0: a_z(0)}
    ay = {0: a_y(0)}
    by = b_y()
    bz = {(0, 0): b_z(0, 0)}
    a_sibs.append(a_sib(0, 0))

    for c in q_far:
        c.wait_recv()
    project(qx, QROWS)

    arrived(az[0])
    az[1], ay[1] = a_z(1), a_y(1)
    arrived(ay[0])
    ayl = {0: a_y_last(0)}
    arrived(by)
    byl = b_y_last()
    bz[1, 0] = b_z(1, 0)
    arrived(bz[0, 0])
    bz[0, 1] = b_z(0, 1)
    a_sibs += [a_sib(0, 1), a_sib(1, 0), a_sib(2, 0)]

    q_at = lax.broadcasted_iota(jnp.int32, (QROWS, QROWS), 0)
    k_at = lax.broadcasted_iota(jnp.int32, (QROWS, QROWS), 1)
    q_seen = (k_at <= q_at) & (lax.div(q_at, QLEN) == lax.div(k_at, QLEN))
    for h in range(HEADS):
        queries = turned(acc[pl.ds(0, QROWS), h * 384 : h * 384 + 128], QROWS, PROWS)
        keys = turned(acc[pl.ds(0, QROWS), h * 384 + 128 : h * 384 + 256], QROWS, PROWS)
        values = acc[pl.ds(0, QROWS), h * 384 + 256 : h * 384 + 384].astype(jnp.bfloat16)
        qk[h], qv[h] = keys, values
        scores = jnp.where(q_seen, dot_nt(queries, keys) * scale, -1e30)
        peak = jnp.max(scores, axis=-1, keepdims=True)
        expon = jnp.where(q_seen, jnp.exp(scores - peak), 0.0)
        weights = (expon / jnp.sum(expon, axis=-1, keepdims=True)).astype(jnp.bfloat16)
        own = jnp.dot(weights, values, preferred_element_type=jnp.float32)
        qo_ref[:, h * HD : (h + 1) * HD] = own.astype(jnp.bfloat16)

    arrived(az[1])
    az[2], ay[2] = a_z(2), a_y(2)
    arrived(ay[1])
    ayl[1] = a_y_last(1)
    arrived(byl)
    bz[2, 0] = b_z(2, 0)
    arrived(bz[1, 0])
    bz[1, 1] = b_z(1, 1)
    arrived(bz[0, 1])
    bz[0, 2] = b_z(0, 2)
    arrived(ayl[0])
    b_sibs.append(b_sib(0))
    a_sibs += [a_sib(0, 2), a_sib(1, 1), a_sib(2, 1), a_sib(3, 0)]

    arrived(az[2])
    az[3], ay[3] = a_z(3), a_y(3)
    arrived(ay[2])
    ayl[2] = a_y_last(2)
    arrived(bz[2, 0])
    bz[2, 1] = b_z(2, 1)
    arrived(bz[1, 1])
    bz[1, 2] = b_z(1, 2)
    arrived(bz[0, 2])
    bz[0, 3] = b_z(0, 3)
    arrived(ayl[1])
    b_sibs.append(b_sib(1))
    a_sibs += [a_sib(0, 3), a_sib(1, 2), a_sib(2, 2), a_sib(3, 1)]

    arrived(az[3])
    ay[4] = a_y(4)
    arrived(ay[3])
    ayl[3] = a_y_last(3)
    arrived(bz[2, 1])
    bz[2, 2] = b_z(2, 2)
    arrived(bz[1, 2])
    bz[1, 3] = b_z(1, 3)
    arrived(ayl[2])
    b_sibs.append(b_sib(2))
    a_sibs += [a_sib(0, 4), a_sib(1, 3), a_sib(2, 3), a_sib(3, 2)]

    arrived(ay[4])
    ayl[4] = a_y_last(4)
    arrived(bz[2, 2])
    bz[2, 3] = b_z(2, 3)
    arrived(bz[0, 3])
    arrived(bz[1, 3])
    arrived(ayl[3])
    b_sibs.append(b_sib(3))
    a_sibs += [a_sib(1, 4), a_sib(2, 4), a_sib(3, 3)]

    arrived(ayl[4])
    a_sibs.append(a_sib(3, 4))
    arrived(bz[2, 3])
    b_sibs.append(b_sib(4))

    lane = lax.div(lax.broadcasted_iota(jnp.int32, (8, 128), 1), PLEN)
    first_row = lax.broadcasted_iota(jnp.int32, (QLEN, CANDS * PLEN), 0)
    ones = jnp.where(
        lax.broadcasted_iota(jnp.int32, (QLEN, HD), 0) < 2, 1.0, 0.0
    ).astype(jnp.bfloat16)

    def place(m):
        passage = cand_ref[m]
        holder = lax.div(passage, 2)
        dz = lax.rem(lax.div(holder, 8) - z + NZ, NZ)
        dy = lax.rem(lax.rem(lax.div(holder, 2), NY) - y + NY, NY)
        zs = dz * 2 - 1 + lax.div(7 - dz, 7) + lax.div(dz, 5) * (17 - 4 * dz)
        ys = dy * 2 - 1 + lax.div(3 - dy, 3) + lax.div(dy, 3) * (9 - 4 * dy)
        other = lax.rem(holder, 2) - core
        return other * other, ys, zs, lax.rem(passage, 2)

    def fetch(where, slots, from_place, part, stat_at):
        @pl.loop(0, PAIRS)
        def _(m):
            half, ys, zs, pos = place(m)
            slot = from_place(half, ys, zs)
            to = pl.ds(pl.multiple_of(m * PLEN, PLEN), PLEN)
            for name, unit in slots.items():
                block = where[slot, pl.ds(unit * 4 + pos * 2, 2)].reshape(PLEN, HD)
                into = got_q if name[0] == "q" else got_o
                into[int(name[1]), to, :] = block
            both = where[slot, stat_at].astype(jnp.float32)
            second = pos.astype(jnp.float32)
            stats[part, m] = both[:8] * (1.0 - second) + both[8:] * second

    def attend(part):
        for q in range(2):
            thirds = []
            for v in range(3):
                block = stats[part, q * CANDS + 4 * v]
                for j in range(1, 4):
                    block = jnp.where(lane == j, stats[part, q * CANDS + 4 * v + j], block)
                thirds.append(block)
            levels = jnp.concatenate(thirds, axis=1)
            rows = pl.ds(q * CANDS * PLEN, CANDS * PLEN)
            for i in range(2):
                h = 2 * part + i
                level = levels[2 * i : 2 * i + 1] + levels[2 * i + 1 : 2 * i + 2]
                scores = dot_nt(qk[h, pl.ds(q * QLEN, QLEN), :], got_q[h, rows, :]) * scale
                peak = jnp.maximum(jnp.max(scores, axis=0, keepdims=True), level)
                expon = jnp.exp(scores - peak)
                rest = jnp.exp(level - peak)
                whole = jnp.sum(expon, axis=0, keepdims=True) + rest
                weights = (expon / whole).astype(jnp.bfloat16)
                share = rest / whole
                coarse = share.astype(jnp.bfloat16).astype(jnp.float32)
                share = jnp.where(
                    first_row == 0, coarse, jnp.where(first_row == 1, share - coarse, 0.0)
                ).astype(jnp.bfloat16)
                out = dot_tn(weights, qv[h, pl.ds(q * QLEN, QLEN), :])
                out = out + dot_tn(share, ones) * got_o[h, rows, :].astype(jnp.float32)
                po_ref[rows, h * HD : (h + 1) * HD] = out.astype(jnp.bfloat16)

    arrived(a_sibs)
    fetch(ga, A_AT, lambda half, ys, zs: half * 32 + ys * 8 + zs, 0, A_TILES - 1)
    attend(0)
    arrived(b_sibs)
    fetch(gb, B_AT, lambda half, ys, zs: half * 32 + zs * 4 + ys, 1, B_TILES - 1)
    attend(1)

    for c in made:
        c.wait_send()


def local(query_embeds, passage_embeds, passage_lengths, cand_passage, norm_gain, w_qkv):
    bf16, f32 = jnp.bfloat16, jnp.float32
    vmem = pl.BlockSpec(memory_space=pltpu.VMEM)
    smem = pl.BlockSpec(memory_space=pltpu.SMEM)
    query_attn, passage_attn = pl.pallas_call(
        kernel,
        out_shape=(
            jax.ShapeDtypeStruct((QROWS, HEADS * HD), bf16),
            jax.ShapeDtypeStruct((PAIRS * PLEN, HEADS * HD), bf16),
        ),
        in_specs=[smem, smem, vmem, vmem, vmem, vmem, pl.BlockSpec(memory_space=pl.ANY)],
        out_specs=(vmem, vmem),
        scratch_shapes=[
            pltpu.VMEM((4, PROWS, DPART), bf16),
            pltpu.VMEM((4, QROWS, DPART), bf16),
            pltpu.VMEM((D, HEADS, 384), bf16),
            pltpu.VMEM((D, HEADS * 384), bf16),
            pltpu.VMEM((PROWS, HEADS * 384), f32),
            pltpu.VMEM((4, 1, DPART), f32),
            pltpu.VMEM((64, A_TILES, 16, HD), bf16),
            pltpu.VMEM((64, B_TILES, 16, HD), bf16),
            pltpu.VMEM((HEADS, PAIRS * PLEN, HD), bf16),
            pltpu.VMEM((HEADS, PAIRS * PLEN, HD), bf16),
            pltpu.VMEM((2, PAIRS, 8, 128), f32),
            pltpu.VMEM((HEADS, QROWS, HD), bf16),
            pltpu.VMEM((HEADS, QROWS, HD), bf16),
            pltpu.SemaphoreType.DMA((W_CUTS,)),
            pltpu.SemaphoreType.DMA((N_SEMS,)),
            pltpu.SemaphoreType.DMA((N_SEMS,)),
        ],
        compiler_params=pltpu.CompilerParams(
            collective_id=0, has_side_effects=True, vmem_limit_bytes=56 * 2**20
        ),
    )(
        passage_lengths,
        cand_passage,
        query_embeds.reshape(QROWS, DPART),
        passage_embeds.reshape(PROWS, DPART),
        norm_gain,
        jnp.asarray(tables()),
        w_qkv,
    )
    return (
        query_attn.reshape(2, QLEN, HEADS * HD),
        passage_attn.reshape(PAIRS, PLEN, HEADS * HD),
    )


def solution(mesh):
    in_specs = (
        P("store", None, "tp"),
        P("store", None, "tp"),
        P("store"),
        P("store"),
        P(),
        P(None, "tp", None),
    )
    out_specs = (P("store", None, "tp"), P("store", None, "tp"))
    return jax.shard_map(local, mesh=mesh, in_specs=in_specs, out_specs=out_specs, check_vma=False)
```
